32 devices in a mesh: phase: 4 (over x, core), fsdp: 8 (over z, y).
Axes of the slice: x: 2, y: 2, z: 4, core: 2. Of those that a mesh axis runs over, the one named last changes fastest.
Arguments:
- inputs: bfloat16 [2, 512, 8192], P(None, 'fsdp'), may hold values from -6 to 6
- cotangent: bfloat16 [2, 512, 8192], P(None, 'fsdp'), may hold values from -0.059814453 to 0.059814453
- norm_gain: float32 [4, 8192], P('phase'), may hold values from 0.1 to 1.9
- blocks: bfloat16 [4, 1024, 4096], P('phase', 'fsdp'), may hold values from -0.09375 to 0.09375
- first_moment: float32 [4, 1024, 4096], P('phase', 'fsdp'), may hold values from -9 to 9
- second_moment: float32 [4, 1024, 4096], P('phase', 'fsdp'), may hold values from 0.25 to 4
- row_index: int32 [4, 1024], P('phase', 'fsdp'), may hold values from 0 to 127, as said below
- col_index: int32 [4, 1024], P('phase', 'fsdp'), may hold values from 0 to 15, as said below
- delays: int32 [4], P('phase'), may hold values from 1 to 4
Outputs:
- weight_grad: float32 [4, 1024, 4096], P('phase', 'fsdp')
- gain_grad: float32 [4, 8192], P('phase')
The draws below stay inside these ranges and needn't reach their ends.
Inputs may be any that keep to these rules, and one draw needn't show every extreme that they name: Within each section the pairs (row_index, col_index) are distinct, so each section has exactly 1024 of its block positions filled. `col_index`: paired with row_index as above.
All inputs are finite; a program needn't handle non-finite values.
Results may differ from the reference program's by a relative error of at most 0.025.
Values may be sent and summed in bfloat16 or wider, within the bound.
A program may use at most 192 MiB of HBM per device.

```python
import math
import jax
import jax.numpy as jnp
from jax import lax

D = 8192
R = 1024
BLK = 64
MICRO = 2
TOK_DEV = 64
TOKENS = 512
PHASES = 4
NB = 1024
N_FSDP = 8


def block_positions(key):
    phase_keys = jax.random.split(jax.random.fold_in(key, 17), PHASES)

    def one_phase(phase_key):
        return jax.random.permutation(phase_key, 2 * NB)[:NB]
    return jax.vmap(one_phase)(phase_keys).astype(jnp.int32)


def draw_row_index(key, part):
    return block_positions(key) // (R // BLK)


def draw_col_index(key, part):
    return block_positions(key) % (R // BLK)


def plant(array, key, low, top_value):
    extent = array.shape
    index_at = [jax.random.randint(jax.random.fold_in(key, axis), (), 0, extent[axis]) for axis in range(len(extent))]
    array = array.at[tuple(index_at)].set(low)
    longest = extent.index(max(extent))
    index_at[longest] = (index_at[longest] + 1) % extent[longest]
    return array.at[tuple(index_at)].set(top_value)


def level_of(key, shape, cuts, smallest, top_value):
    def one(dim, blocks):
        steps = jax.random.uniform(jax.random.fold_in(jax.random.fold_in(key, 6), dim), (blocks,), jnp.float32, smallest / len(cuts), top_value / len(cuts))
        return jnp.repeat(jnp.exp(steps), shape[dim] // blocks).reshape((-1,) + (1,) * (len(shape) - dim - 1))

    loudness = one(*cuts[0])
    for cut in cuts[1:]:
        loudness = loudness * one(*cut)
    return loudness


def bell_draw(rng, extent, scale, bound, cuts=(), kind=jnp.bfloat16):
    array = jax.random.normal(rng, extent, jnp.float32) * scale
    if len(cuts) > 0:
        array = level_of(rng, extent, cuts, -0.22, 0.18) * array
    return jnp.clip(array, min=-bound, max=bound).astype(kind)


def setup_inputs(seed: int = 0) -> dict:
    seeds = jax.random.split(jax.random.key(seed), 10)
    inputs = bell_draw(seeds[0], (MICRO, TOKENS, D), 1.0, 6.0, ((1, 8),))
    cotangent = bell_draw(seeds[1], (MICRO, TOKENS, D), 0.01, 0.059814453, ((1, 8),))
    norm_gain = jnp.clip(1.0 + 0.18 * jax.random.normal(seeds[2], (PHASES, D), jnp.float32), 0.1, 1.9)
    blocks = bell_draw(seeds[3], (PHASES, NB, BLK * BLK), (D // 2) ** -0.5, 0.09375, ((0, 4), (1, 8)))
    first_moment = bell_draw(seeds[4], (PHASES, NB, BLK * BLK), 1.5, 9.0, ((0, 4), (1, 8)), jnp.float32)
    second_moment = jnp.clip(jnp.exp(math.log(4.0) - 2.7725887 * jax.random.uniform(seeds[5], (PHASES, NB, BLK * BLK), jnp.float32) ** level_of(seeds[5], (PHASES, NB, BLK * BLK), ((0, 4), (1, 8)), -0.2, 0.2)), 0.25, 4.0)
    row_index = draw_row_index(jax.random.fold_in(seeds[9], 71), 0)
    col_index = draw_col_index(jax.random.fold_in(seeds[9], 71), 0)
    delays = plant(jax.random.randint(seeds[8], (PHASES,), 1, PHASES + 1), jax.random.fold_in(seeds[8], 1), 1, PHASES).astype(jnp.int32)
    return {"inputs": inputs, "cotangent": cotangent, "norm_gain": norm_gain, "blocks": blocks, "first_moment": first_moment, "second_moment": second_moment, "row_index": row_index, "col_index": col_index, "delays": delays}


learn_rate = 0.002
adam_epsilon = 1e-08
norm_epsilon = 1e-05

def extrapolate(tile_rows, moment_one, moment_two, delay):
    step_size = learn_rate * delay.astype(jnp.float32)
    moved = tile_rows.astype(jnp.float32) - step_size * moment_one / (jnp.sqrt(moment_two) + adam_epsilon)
    return moved.astype(jnp.bfloat16)

def assemble(tile_rows, row_pick, col_pick):
    stacked = tile_rows.reshape(tile_rows.shape[0], BLK, BLK)
    tile_grid = jnp.zeros((D // BLK, R // BLK, BLK, BLK), stacked.dtype)
    tile_grid = tile_grid.at[row_pick, col_pick].set(stacked)
    return tile_grid.transpose(0, 2, 1, 3).reshape(D, R)

def transpose_product(left_side, matrix):
    return lax.dot_general(left_side, matrix, (((1,), (1,)), ((), ())), preferred_element_type=jnp.float32)

def block_terms(left_cat, right_cat, row_pick, col_pick):
    left_tiles = left_cat.reshape(left_cat.shape[0], D // BLK, BLK)
    right_tiles = right_cat.reshape(right_cat.shape[0], R // BLK, BLK)
    block_total = row_pick.shape[0]
    group_size = math.gcd(block_total, 64)

    def one_group(group_id):
        rows_now = lax.dynamic_slice_in_dim(row_pick, group_id * group_size, group_size)
        cols_now = lax.dynamic_slice_in_dim(col_pick, group_id * group_size, group_size)
        left_rows = jnp.take(left_tiles, rows_now, axis=1).astype(jnp.float32)
        right_rows = jnp.take(right_tiles, cols_now, axis=1).astype(jnp.float32)
        product = jnp.einsum('tni,tnj->nij', left_rows, right_rows)
        return product.reshape(group_size, BLK * BLK)
    results = lax.map(one_group, jnp.arange(block_total // group_size, dtype=jnp.int32))
    return results.reshape(block_total, BLK * BLK)

def normalize(phase_in, gain_row):
    x_float = phase_in.astype(jnp.float32)
    rms_scale = lax.rsqrt(lax.optimization_barrier(jnp.mean(x_float * x_float, axis=-1, keepdims=True)) + norm_epsilon)
    normed = x_float * rms_scale
    hidden = (normed * gain_row).astype(jnp.bfloat16)
    return (x_float, rms_scale, normed, hidden)

def by_group(pieces):
    stacked = jnp.stack(pieces)
    width = stacked.shape[-1]
    grouped = stacked.reshape(MICRO, N_FSDP, TOK_DEV, width).transpose(1, 0, 2, 3)
    return grouped.reshape(N_FSDP, MICRO * TOK_DEV, width)

def group_grads(hidden_list, grad_list, dpre_list, act_list, row_pick, col_pick):
    operands = (by_group(hidden_list), by_group(grad_list), by_group(dpre_list), by_group(act_list))

    def one_device(total, pieces):
        hidden_g, grad_g, dpre_g, act_g = pieces
        left_cat = jnp.concatenate([hidden_g, grad_g], axis=0)
        right_cat = jnp.concatenate([dpre_g, act_g], axis=0)
        term = block_terms(left_cat, right_cat, row_pick, col_pick)
        rounded = lax.optimization_barrier(term.astype(jnp.bfloat16)).astype(jnp.float32)
        return (total + rounded, None)
    total, unused = lax.scan(one_device, jnp.zeros((row_pick.shape[0], BLK * BLK), jnp.float32), operands)
    return total

def reference(inputs, cotangent, norm_gain, blocks, first_moment, second_moment, row_index, col_index, delays):
    matrices = []
    for phase_num in range(PHASES):
        moved = extrapolate(blocks[phase_num], first_moment[phase_num], second_moment[phase_num], delays[phase_num])
        matrices.append(assemble(moved, row_index[phase_num], col_index[phase_num]))
    saved = {}
    for batch_id in range(MICRO):
        phase_in = inputs[batch_id]
        for phase_num in range(PHASES):
            x_float, rms_scale, normed, hidden = normalize(phase_in, norm_gain[phase_num])
            pre_act = jnp.dot(hidden, matrices[phase_num], preferred_element_type=jnp.float32)
            act_out = jax.nn.silu(pre_act).astype(jnp.bfloat16)
            saved[phase_num, batch_id] = (phase_in, pre_act, act_out)
            phase_in = (x_float + transpose_product(act_out, matrices[phase_num])).astype(jnp.bfloat16)
    gain_grads = [jnp.zeros((D,), jnp.float32) for phase_num in range(PHASES)]
    kept = {}
    for batch_id in range(MICRO):
        grad_out = cotangent[batch_id]
        for phase_num in reversed(range(PHASES)):
            phase_in, pre_act, act_out = saved[phase_num, batch_id]
            x_float, rms_scale, normed, hidden = normalize(phase_in, norm_gain[phase_num])
            dact = jnp.dot(grad_out, matrices[phase_num], preferred_element_type=jnp.float32)
            sigmoid_pre = jax.nn.sigmoid(pre_act)
            dpre = (dact * sigmoid_pre * (1.0 + pre_act * (1.0 - sigmoid_pre))).astype(jnp.bfloat16)
            dhidden = transpose_product(dpre, matrices[phase_num])
            gain_grads[phase_num] = gain_grads[phase_num] + lax.optimization_barrier(jnp.sum(dhidden * normed, axis=0))
            kept[phase_num, batch_id] = (hidden, grad_out, dpre, act_out)
            dnormed = dhidden * norm_gain[phase_num]
            inner = lax.optimization_barrier(jnp.mean(dnormed * normed, axis=-1, keepdims=True))
            grad_out = (grad_out.astype(jnp.float32) + rms_scale * (dnormed - normed * inner)).astype(jnp.bfloat16)
    weight_grads = []
    for phase_num in range(PHASES):
        hidden_list = [kept[phase_num, batch_id][0] for batch_id in range(MICRO)]
        grad_list = [kept[phase_num, batch_id][1] for batch_id in range(MICRO)]
        dpre_list = [kept[phase_num, batch_id][2] for batch_id in range(MICRO)]
        act_list = [kept[phase_num, batch_id][3] for batch_id in range(MICRO)]
        weight_grads.append(group_grads(hidden_list, grad_list, dpre_list, act_list, row_index[phase_num], col_index[phase_num]))
    return (jnp.stack(weight_grads), jnp.stack(gain_grads))
```

```python
import functools

import jax
import jax.numpy as jnp
from jax import lax
from jax.experimental import pallas as pl
from jax.experimental.pallas import tpu as pltpu
from jax.sharding import PartitionSpec as P

D = 8192
R = 1024
BLK = 64
VMEM_BYTES = 56 * 2**20


learn_rate = 0.002
adam_epsilon = 1e-08
norm_epsilon = 1e-05


def shifted(value, axis, steps):
    count = lax.axis_size(axis)
    initial, last = (max(0, -steps), min(count, count - steps))
    return lax.ppermute(value, axis, [(source, source + steps) for source in range(initial, last)])


def extrapolate(tile_rows, moment_one, moment_two, delay):
    step_size = learn_rate * delay.astype(jnp.float32)
    moved = tile_rows.astype(jnp.float32) - step_size * moment_one / (
        jnp.sqrt(moment_two) + adam_epsilon
    )
    return moved.astype(jnp.bfloat16)


def pack_pairs(tile_rows):
    half = tile_rows.shape[0] // 2
    halves = tile_rows.reshape(2, half, BLK, BLK)
    return halves.transpose(1, 2, 0, 3).reshape(half, BLK, 2 * BLK)


def unpack_pairs(pairs):
    half = pairs.shape[0]
    halves = pairs.reshape(half, BLK, 2, BLK).transpose(2, 0, 1, 3)
    return halves.reshape(2 * half, BLK * BLK)


def swap_halves(value):
    return jnp.concatenate([value[:, BLK:], value[:, :BLK]], axis=1)


def lane_half():
    return lax.broadcasted_iota(jnp.int32, (BLK, 2 * BLK), 1) // BLK


def block_numbers(pair, half):
    first = (pair // half) * (2 * half) + pair % half
    return (first, first + half)


def assemble_kernel(half, rows_ref, cols_ref, pairs_ref, out_ref):
    @pl.loop(0, D // 512)
    def _(chunk):
        out_ref[pl.ds(pl.multiple_of(chunk * 512, 512), 512), :] = jnp.zeros((512, R), jnp.bfloat16)

    @pl.loop(0, pairs_ref.shape[0], unroll=4)
    def _(pair):
        straight = pairs_ref[pair]
        swapped = swap_halves(straight)
        for side, number in enumerate(block_numbers(pair, half)):
            row, col = rows_ref[number], cols_ref[number]
            parity = col % 2
            at = (
                pl.ds(pl.multiple_of(row * BLK, BLK), BLK),
                pl.ds(pl.multiple_of((col // 2) * 2 * BLK, 2 * BLK), 2 * BLK),
            )
            tile = jnp.where(parity == side, straight, swapped)
            out_ref[at] = jnp.where(lane_half() == parity, tile, out_ref[at])


def assemble(pairs, row_pick, col_pick, half):
    return pl.pallas_call(
        functools.partial(assemble_kernel, half),
        out_shape=jax.ShapeDtypeStruct((D, R), jnp.bfloat16),
        in_specs=[pl.BlockSpec(memory_space=pltpu.SMEM)] * 2
        + [pl.BlockSpec(memory_space=pltpu.VMEM)],
        out_specs=pl.BlockSpec(memory_space=pltpu.VMEM),
        compiler_params=pltpu.CompilerParams(vmem_limit_bytes=VMEM_BYTES),
        name="assemble",
    )(row_pick, col_pick, pairs)


def grads_kernel(half, rows_ref, cols_ref, left_ref, right_ref, out_ref, dense):
    @pl.loop(0, D // 512)
    def _(chunk):
        at = pl.ds(pl.multiple_of(chunk * 512, 512), 512)
        dense[at, :] = lax.dot_general(
            left_ref[:, at],
            right_ref[...],
            (((0,), (0,)), ((), ())),
            preferred_element_type=jnp.float32,
        ).astype(jnp.bfloat16)

    @pl.loop(0, out_ref.shape[0], unroll=4)
    def _(pair):
        tiles = []
        for side, number in enumerate(block_numbers(pair, half)):
            row, col = rows_ref[number], cols_ref[number]
            tile = dense[
                pl.ds(pl.multiple_of(row * BLK, BLK), BLK),
                pl.ds(pl.multiple_of((col // 2) * 2 * BLK, 2 * BLK), 2 * BLK),
            ]
            tiles.append(jnp.where(col % 2 == side, tile, swap_halves(tile)))
        out_ref[pair] = jnp.where(lane_half() == 0, tiles[0], tiles[1])


def block_grads(left_cat, right_cat, row_pick, col_pick, half):
    pairs = row_pick.shape[0] // 2
    return pl.pallas_call(
        functools.partial(grads_kernel, half),
        out_shape=jax.ShapeDtypeStruct((pairs, BLK, 2 * BLK), jnp.bfloat16),
        in_specs=[pl.BlockSpec(memory_space=pltpu.SMEM)] * 2
        + [pl.BlockSpec(memory_space=pltpu.VMEM)] * 2,
        out_specs=pl.BlockSpec(memory_space=pltpu.VMEM),
        scratch_shapes=[pltpu.VMEM((D, R), jnp.bfloat16)],
        compiler_params=pltpu.CompilerParams(vmem_limit_bytes=VMEM_BYTES),
        name="block_grads",
    )(row_pick, col_pick, left_cat, right_cat)


def transpose_product(left_side, matrix):
    return lax.dot_general(
        left_side, matrix, (((1,), (1,)), ((), ())), preferred_element_type=jnp.float32
    )


def make_products(pairs, row_pick, col_pick, half):
    matrix = assemble(pairs, row_pick, col_pick, half)

    def times_matrix(left_side):
        return jnp.dot(left_side, matrix, preferred_element_type=jnp.float32)

    def times_transpose(left_side):
        return transpose_product(left_side, matrix)

    return (times_matrix, times_transpose)


def normalize(phase_in, gain_row):
    x_float = phase_in.astype(jnp.float32)
    rms_scale = lax.rsqrt(jnp.mean(x_float * x_float, axis=-1, keepdims=True) + norm_epsilon)
    normed = x_float * rms_scale
    hidden = (normed * gain_row).astype(jnp.bfloat16)
    return (x_float, rms_scale, normed, hidden)


def shards(
    inputs, cotangent, norm_gain, blocks, first_moment, second_moment, row_index, col_index, delays
):
    phases = lax.axis_size("phase")
    phase_id = lax.axis_index("phase")
    micro_count, tok_rows, model_width = inputs.shape
    gain_row = norm_gain[0]
    local_blocks = extrapolate(blocks[0], first_moment[0], second_moment[0], delays[0])
    half = local_blocks.shape[0] // 2
    all_pairs = lax.all_gather(pack_pairs(local_blocks), "fsdp", axis=0, tiled=True)
    positions = lax.all_gather(
        jnp.stack([row_index[0], col_index[0]]), "fsdp", axis=1, tiled=True
    )
    all_rows, all_cols = positions[0], positions[1]
    forward_matrix, forward_transpose = make_products(all_pairs, all_rows, all_cols, half)
    tick_count = micro_count + phases - 1

    def forward_compute(tick, incoming, stores):
        batch_index = tick - phase_id
        is_valid = (batch_index >= 0) & (batch_index < micro_count)
        batch_slot = jnp.clip(batch_index, 0, micro_count - 1)
        first_input = lax.dynamic_index_in_dim(inputs, batch_slot, 0, keepdims=False)
        phase_in = jnp.where(phase_id == 0, first_input, incoming)

        def compute(operands):
            phase_in, stores = operands
            x_all, hidden_all, pre_all, act_all = stores
            x_float, rms_scale, normed, hidden = normalize(phase_in, gain_row)
            pre_act = forward_matrix(hidden)
            act_out = jax.nn.silu(pre_act).astype(jnp.bfloat16)
            phase_out = (x_float + forward_transpose(act_out)).astype(jnp.bfloat16)
            x_all = lax.dynamic_update_index_in_dim(x_all, phase_in, batch_slot, 0)
            hidden_all = lax.dynamic_update_index_in_dim(hidden_all, hidden, batch_slot, 0)
            pre_all = lax.dynamic_update_index_in_dim(pre_all, pre_act, batch_slot, 0)
            act_all = lax.dynamic_update_index_in_dim(act_all, act_out, batch_slot, 0)
            return (phase_out, (x_all, hidden_all, pre_all, act_all))

        def forward_passing(operands):
            return operands

        return lax.cond(is_valid, compute, forward_passing, (phase_in, stores))

    def forward_tick(tick, state_carry):
        incoming, stores = state_carry
        phase_out, stores = forward_compute(tick, incoming, stores)
        incoming = shifted(phase_out, "phase", 1)
        return (incoming, stores)

    forward_init = (
        jnp.zeros((micro_count, tok_rows, model_width), jnp.bfloat16),
        jnp.zeros((micro_count, tok_rows, model_width), jnp.bfloat16),
        jnp.zeros((micro_count, tok_rows, R), jnp.float32),
        jnp.zeros((micro_count, tok_rows, R), jnp.bfloat16),
    )
    forward_carry = lax.fori_loop(
        0,
        tick_count - 1,
        forward_tick,
        (jnp.zeros((tok_rows, model_width), jnp.bfloat16), forward_init),
    )
    unused_out, forward_done = forward_compute(tick_count - 1, forward_carry[0], forward_carry[1])
    x_all, hidden_all, pre_all, act_all = forward_done
    back_matrix, back_transpose = (forward_matrix, forward_transpose)

    def backward_compute(tick, incoming, stores):
        batch_index = tick - (phases - 1 - phase_id)
        is_valid = (batch_index >= 0) & (batch_index < micro_count)
        batch_slot = jnp.clip(batch_index, 0, micro_count - 1)
        last_grad = lax.dynamic_index_in_dim(cotangent, batch_slot, 0, keepdims=False)
        grad_out = jnp.where(phase_id == phases - 1, last_grad, incoming)

        def compute(operands):
            grad_out, stores = operands
            grad_all, dpre_all, gain_total = stores
            phase_in = lax.dynamic_index_in_dim(x_all, batch_slot, 0, keepdims=False)
            pre_act = lax.dynamic_index_in_dim(pre_all, batch_slot, 0, keepdims=False)
            x_float, rms_scale, normed, hidden = normalize(phase_in, gain_row)
            dact = back_matrix(grad_out)
            sigmoid_pre = jax.nn.sigmoid(pre_act)
            dpre = (dact * sigmoid_pre * (1.0 + pre_act * (1.0 - sigmoid_pre))).astype(jnp.bfloat16)
            dhidden = back_transpose(dpre)
            gain_total = gain_total + jnp.sum(dhidden * normed, axis=0)
            dnormed = dhidden * gain_row
            inner = jnp.mean(dnormed * normed, axis=-1, keepdims=True)
            grad_in = (
                grad_out.astype(jnp.float32) + rms_scale * (dnormed - normed * inner)
            ).astype(jnp.bfloat16)
            grad_all = lax.dynamic_update_index_in_dim(grad_all, grad_out, batch_slot, 0)
            dpre_all = lax.dynamic_update_index_in_dim(dpre_all, dpre, batch_slot, 0)
            return (grad_in, (grad_all, dpre_all, gain_total))

        def backward_passing(operands):
            return operands

        return lax.cond(is_valid, compute, backward_passing, (grad_out, stores))

    def backward_tick(tick, state_carry):
        incoming, stores = state_carry
        grad_in, stores = backward_compute(tick, incoming, stores)
        incoming = shifted(grad_in, "phase", -1)
        return (incoming, stores)

    backward_init = (
        jnp.zeros((micro_count, tok_rows, model_width), jnp.bfloat16),
        jnp.zeros((micro_count, tok_rows, R), jnp.bfloat16),
        jnp.zeros((model_width,), jnp.float32),
    )
    backward_carry = lax.fori_loop(
        0,
        tick_count - 1,
        backward_tick,
        (jnp.zeros((tok_rows, model_width), jnp.bfloat16), backward_init),
    )
    unused_grad, backward_done = backward_compute(
        tick_count - 1, backward_carry[0], backward_carry[1]
    )
    grad_all, dpre_all, gain_total = backward_done
    token_total = micro_count * tok_rows
    left_cat = jnp.concatenate(
        [hidden_all.reshape(token_total, model_width), grad_all.reshape(token_total, model_width)],
        axis=0,
    )
    right_cat = jnp.concatenate(
        [dpre_all.reshape(token_total, R), act_all.reshape(token_total, R)], axis=0
    )
    parts = block_grads(left_cat, right_cat, all_rows, all_cols, half)
    weight_pairs = lax.psum_scatter(parts, "fsdp", scatter_dimension=0, tiled=True)
    weight_part = unpack_pairs(weight_pairs.astype(jnp.float32))
    gain_part = lax.psum(gain_total.astype(jnp.bfloat16), "fsdp").astype(jnp.float32)
    return (weight_part[None], gain_part[None])


def solution(mesh):
    in_specs = (
        P(None, "fsdp", None),
        P(None, "fsdp", None),
        P("phase", None),
        P("phase", "fsdp", None),
        P("phase", "fsdp", None),
        P("phase", "fsdp", None),
        P("phase", "fsdp"),
        P("phase", "fsdp"),
        P("phase"),
    )
    out_specs = (P("phase", "fsdp", None), P("phase", None))
    return jax.shard_map(shards, mesh=mesh, in_specs=in_specs, out_specs=out_specs, check_vma=False)
```

```python
import functools

import jax
import jax.numpy as jnp
from jax import lax
from jax.experimental import pallas as pl
from jax.experimental.pallas import tpu as pltpu
from jax.sharding import PartitionSpec as P

D = 8192
R = 1024
BLK = 64
CHUNK = 1024
VMEM_BYTES = 56 * 2**20


learn_rate = 0.002
adam_epsilon = 1e-08
norm_epsilon = 1e-05


def extrapolate(tile_rows, moment_one, moment_two, delay):
    step_size = learn_rate * delay.astype(jnp.float32)
    moved = tile_rows.astype(jnp.float32) - step_size * moment_one / (
        jnp.sqrt(moment_two) + adam_epsilon
    )
    return moved.astype(jnp.bfloat16)


def pack_pairs(tile_rows):
    half = tile_rows.shape[0] // 2
    halves = tile_rows.reshape(2, half, BLK, BLK)
    return halves.transpose(1, 2, 0, 3).reshape(half, BLK, 2 * BLK)


def unpack_pairs(pairs):
    half = pairs.shape[0]
    halves = pairs.reshape(half, BLK, 2, BLK).transpose(2, 0, 1, 3)
    return halves.reshape(2 * half, BLK * BLK)


def swap_halves(value):
    return jnp.concatenate([value[:, BLK:], value[:, :BLK]], axis=1)


def lane_half():
    return lax.broadcasted_iota(jnp.int32, (BLK, 2 * BLK), 1) // BLK


def block_numbers(pair, half):
    first = (pair // half) * (2 * half) + pair % half
    return (first, first + half)


def assemble_kernel(half, rows_ref, cols_ref, pairs_ref, out_ref):
    @pl.loop(0, D // 512)
    def _(chunk):
        out_ref[pl.ds(pl.multiple_of(chunk * 512, 512), 512), :] = jnp.zeros((512, R), jnp.bfloat16)

    @pl.loop(0, pairs_ref.shape[0], unroll=4)
    def _(pair):
        straight = pairs_ref[pair]
        swapped = swap_halves(straight)
        for side, number in enumerate(block_numbers(pair, half)):
            row, col = rows_ref[number], cols_ref[number]
            parity = col % 2
            at = (
                pl.ds(pl.multiple_of(row * BLK, BLK), BLK),
                pl.ds(pl.multiple_of((col // 2) * 2 * BLK, 2 * BLK), 2 * BLK),
            )
            tile = jnp.where(parity == side, straight, swapped)
            out_ref[at] = jnp.where(lane_half() == parity, tile, out_ref[at])


def assemble(pairs, row_pick, col_pick, half):
    return pl.pallas_call(
        functools.partial(assemble_kernel, half),
        out_shape=jax.ShapeDtypeStruct((D, R), jnp.bfloat16),
        in_specs=[pl.BlockSpec(memory_space=pltpu.SMEM)] * 2
        + [pl.BlockSpec(memory_space=pltpu.VMEM)],
        out_specs=pl.BlockSpec(memory_space=pltpu.VMEM),
        compiler_params=pltpu.CompilerParams(vmem_limit_bytes=VMEM_BYTES),
        name="assemble",
    )(row_pick, col_pick, pairs)


def grads_kernel(half, rows_ref, cols_ref, left_ref, right_ref, out_ref, dense):
    @pl.loop(0, D // 512)
    def _(chunk):
        at = pl.ds(pl.multiple_of(chunk * 512, 512), 512)
        dense[at, :] = lax.dot_general(
            left_ref[:, at],
            right_ref[...],
            (((0,), (0,)), ((), ())),
            preferred_element_type=jnp.float32,
        ).astype(jnp.bfloat16)

    @pl.loop(0, out_ref.shape[0], unroll=4)
    def _(pair):
        tiles = []
        for side, number in enumerate(block_numbers(pair, half)):
            row, col = rows_ref[number], cols_ref[number]
            tile = dense[
                pl.ds(pl.multiple_of(row * BLK, BLK), BLK),
                pl.ds(pl.multiple_of((col // 2) * 2 * BLK, 2 * BLK), 2 * BLK),
            ]
            tiles.append(jnp.where(col % 2 == side, tile, swap_halves(tile)))
        out_ref[pair] = jnp.where(lane_half() == 0, tiles[0], tiles[1])


def block_grads(left_cat, right_cat, row_pick, col_pick, half):
    pairs = row_pick.shape[0] // 2
    return pl.pallas_call(
        functools.partial(grads_kernel, half),
        out_shape=jax.ShapeDtypeStruct((pairs, BLK, 2 * BLK), jnp.bfloat16),
        in_specs=[pl.BlockSpec(memory_space=pltpu.SMEM)] * 2
        + [pl.BlockSpec(memory_space=pltpu.VMEM)] * 2,
        out_specs=pl.BlockSpec(memory_space=pltpu.VMEM),
        scratch_shapes=[pltpu.VMEM((D, R), jnp.bfloat16)],
        compiler_params=pltpu.CompilerParams(vmem_limit_bytes=VMEM_BYTES),
        name="block_grads",
    )(row_pick, col_pick, left_cat, right_cat)


def relay_kernel(
    phases,
    inputs_ref,
    cotangent_ref,
    gain_ref,
    matrix_ref,
    left_ref,
    right_ref,
    total_ref,
    x_in,
    x_out,
    grad_back,
    pre_all,
    scale_all,
    sums,
    square,
    send_sem,
    recv_sem,
):
    micro_count, tok_rows, width = inputs_ref.shape
    chunks = width // CHUNK
    phase_id = lax.axis_index("phase")
    has_next, has_prev = (phase_id < phases - 1, phase_id > 0)
    after, before = (lax.rem(phase_id + 1, phases), lax.rem(phase_id + phases - 1, phases))
    barrier = pltpu.get_barrier_semaphore()

    for neighbour in (after, before):
        pl.semaphore_signal(
            barrier, inc=1, device_id={"phase": neighbour}, device_id_type=pl.DeviceIdType.MESH
        )

    def span(chunk):
        return pl.ds(pl.multiple_of(chunk * CHUNK, CHUNK), CHUNK)

    def grad_rows(batch):
        return pl.ds((micro_count + batch) * tok_rows, tok_rows)

    def batch_rows(batch):
        return pl.ds(batch * tok_rows, tok_rows)

    def forward_copy(batch, chunk):
        return pltpu.make_async_remote_copy(
            src_ref=x_out.at[batch, :, span(chunk)],
            dst_ref=x_in.at[batch, :, span(chunk)],
            send_sem=send_sem.at[0, batch, chunk],
            recv_sem=recv_sem.at[0, batch, chunk],
            device_id={"phase": after},
            device_id_type=pl.DeviceIdType.MESH,
        )

    def backward_copy(batch, chunk):
        return pltpu.make_async_remote_copy(
            src_ref=x_out.at[micro_count + batch, :, span(chunk)],
            dst_ref=grad_back.at[batch, :, span(chunk)],
            send_sem=send_sem.at[1, batch, chunk],
            recv_sem=recv_sem.at[1, batch, chunk],
            device_id={"phase": before},
            device_id_type=pl.DeviceIdType.MESH,
        )

    @pl.when(jnp.logical_not(has_prev))
    def _():
        x_in[...] = inputs_ref[...]

    @pl.when(jnp.logical_not(has_next))
    def _():
        grad_back[...] = cotangent_ref[...]

    pl.semaphore_wait(barrier, 2)

    for batch in range(micro_count):
        sums[...] = jnp.zeros_like(sums)
        square[...] = jnp.zeros_like(square)

        @pl.loop(0, chunks)
        def _(chunk):
            @pl.when(has_prev)
            def _():
                forward_copy(batch, chunk).wait_recv()

            at = span(chunk)
            x_float = x_in[batch, :, at].astype(jnp.float32)
            weighted = (x_float * gain_ref[:, at]).astype(jnp.bfloat16)
            square[...] += jnp.sum(x_float * x_float, axis=-1, keepdims=True)
            sums[...] += jnp.dot(weighted, matrix_ref[at, :], preferred_element_type=jnp.float32)

        rms_scale = lax.rsqrt(square[...] / width + norm_epsilon)
        pre = sums[...] * rms_scale
        act = (pre / (1.0 + jnp.exp(-pre))).astype(jnp.bfloat16)
        scale_all[batch] = rms_scale
        pre_all[batch] = pre
        right_ref[grad_rows(batch), :] = act

        @pl.when(has_next)
        def _():
            @pl.loop(0, chunks)
            def _(chunk):
                at = span(chunk)
                moved = transpose_product(right_ref[grad_rows(batch), :], matrix_ref[at, :])
                x_out[batch, :, at] = (x_in[batch, :, at].astype(jnp.float32) + moved).astype(
                    jnp.bfloat16
                )
                forward_copy(batch, chunk).start()

    for batch in range(micro_count):
        sums[...] = jnp.zeros_like(sums)

        @pl.loop(0, chunks)
        def _(chunk):
            @pl.when(has_next)
            def _():
                backward_copy(batch, chunk).wait_recv()

            at = span(chunk)
            sums[...] += jnp.dot(
                grad_back[batch, :, at], matrix_ref[at, :], preferred_element_type=jnp.float32
            )

        pre = pre_all[batch]
        sigmoid_pre = 1.0 / (1.0 + jnp.exp(-pre))
        dpre = (sums[...] * sigmoid_pre * (1.0 + pre * (1.0 - sigmoid_pre))).astype(jnp.bfloat16)
        right_ref[batch_rows(batch), :] = dpre
        inner = jnp.sum(dpre.astype(jnp.float32) * pre, axis=-1, keepdims=True) / width
        square[...] = inner

        @pl.loop(0, chunks)
        def _(chunk):
            at = span(chunk)
            dhidden = transpose_product(right_ref[batch_rows(batch), :], matrix_ref[at, :])
            gain_row = gain_ref[:, at]
            rms_scale = scale_all[batch]
            normed = x_in[batch, :, at].astype(jnp.float32) * rms_scale
            grad_out = grad_back[batch, :, at]
            x_out[micro_count + batch, :, at] = (
                grad_out.astype(jnp.float32)
                + rms_scale * (dhidden * gain_row - normed * square[...])
            ).astype(jnp.bfloat16)

            @pl.when(has_prev)
            def _():
                backward_copy(batch, chunk).start()

            gain_part = jnp.sum(dhidden * normed, axis=0, keepdims=True)
            if batch == 0:
                total_ref[:, at] = gain_part
            else:
                total_ref[:, at] += gain_part
            left_ref[batch_rows(batch), at] = (normed * gain_row).astype(jnp.bfloat16)
            left_ref[grad_rows(batch), at] = grad_out

    @pl.loop(0, chunks)
    def _(chunk):
        for batch in range(micro_count):
            @pl.when(has_next)
            def _():
                forward_copy(batch, chunk).wait_send()

            @pl.when(has_prev)
            def _():
                backward_copy(batch, chunk).wait_send()


def relay(inputs, cotangent, norm_gain, matrix):
    micro_count, tok_rows, width = inputs.shape
    inner = matrix.shape[1]
    vmem = pl.BlockSpec(memory_space=pltpu.VMEM)
    rows = 2 * micro_count * tok_rows
    return pl.pallas_call(
        functools.partial(relay_kernel, lax.axis_size("phase")),
        out_shape=(
            jax.ShapeDtypeStruct((rows, width), jnp.bfloat16),
            jax.ShapeDtypeStruct((rows, inner), jnp.bfloat16),
            jax.ShapeDtypeStruct((1, width), jnp.float32),
        ),
        in_specs=[vmem] * 4,
        out_specs=(vmem,) * 3,
        scratch_shapes=[
            pltpu.VMEM((micro_count, tok_rows, width), jnp.bfloat16),
            pltpu.VMEM((2 * micro_count, tok_rows, width), jnp.bfloat16),
            pltpu.VMEM((micro_count, tok_rows, width), jnp.bfloat16),
            pltpu.VMEM((micro_count, tok_rows, inner), jnp.float32),
            pltpu.VMEM((micro_count, tok_rows, 1), jnp.float32),
            pltpu.VMEM((tok_rows, inner), jnp.float32),
            pltpu.VMEM((tok_rows, 1), jnp.float32),
            pltpu.SemaphoreType.DMA((2, micro_count, width // CHUNK)),
            pltpu.SemaphoreType.DMA((2, micro_count, width // CHUNK)),
        ],
        compiler_params=pltpu.CompilerParams(
            vmem_limit_bytes=VMEM_BYTES, collective_id=0, has_side_effects=True
        ),
        name="relay",
    )(inputs, cotangent, norm_gain, matrix)


def transpose_product(left_side, matrix):
    return lax.dot_general(
        left_side, matrix, (((1,), (1,)), ((), ())), preferred_element_type=jnp.float32
    )


def shards(
    inputs, cotangent, norm_gain, blocks, first_moment, second_moment, row_index, col_index, delays
):
    local_blocks = extrapolate(blocks[0], first_moment[0], second_moment[0], delays[0])
    half = local_blocks.shape[0] // 2
    all_pairs = lax.all_gather(pack_pairs(local_blocks), "fsdp", axis=0, tiled=True)
    positions = lax.all_gather(
        jnp.stack([row_index[0], col_index[0]]), "fsdp", axis=1, tiled=True
    )
    all_rows, all_cols = positions[0], positions[1]
    matrix = assemble(all_pairs, all_rows, all_cols, half)
    left_cat, right_cat, gain_total = relay(inputs, cotangent, norm_gain, matrix)
    parts = block_grads(left_cat, right_cat, all_rows, all_cols, half)
    weight_pairs = lax.psum_scatter(parts, "fsdp", scatter_dimension=0, tiled=True)
    weight_part = unpack_pairs(weight_pairs.astype(jnp.float32))
    gain_part = lax.psum(gain_total[0].astype(jnp.bfloat16), "fsdp").astype(jnp.float32)
    return (weight_part[None], gain_part[None])


def solution(mesh):
    in_specs = (
        P(None, "fsdp", None),
        P(None, "fsdp", None),
        P("phase", None),
        P("phase", "fsdp", None),
        P("phase", "fsdp", None),
        P("phase", "fsdp", None),
        P("phase", "fsdp"),
        P("phase", "fsdp"),
        P("phase"),
    )
    out_specs = (P("phase", "fsdp", None), P("phase", None))
    return jax.shard_map(shards, mesh=mesh, in_specs=in_specs, out_specs=out_specs, check_vma=False)
```

```python
import functools

import jax
import jax.numpy as jnp
from jax import lax
from jax.experimental import pallas as pl
from jax.experimental.pallas import tpu as pltpu
from jax.sharding import PartitionSpec as P

D = 8192
R = 1024
BLK = 64
CHUNK = 1024
VMEM_BYTES = 56 * 2**20


learn_rate = 0.002
adam_epsilon = 1e-08
norm_epsilon = 1e-05


def lane_join(low, high):
    return jnp.concatenate([low, high], axis=1)


def pack_kernel(delay_ref, tiles_ref, one_ref, two_ref, out_ref, wide):
    half = tiles_ref.shape[0] // 2
    step_size = learn_rate * delay_ref[0].astype(jnp.float32)
    for step in range(BLK // 2):
        at = slice(step * 2 * BLK, (step + 1) * 2 * BLK)
        moved = tiles_ref[:, at].astype(jnp.float32) - step_size * one_ref[:, at] / (
            jnp.sqrt(two_ref[:, at]) + adam_epsilon
        )
        low, high = moved[:half], moved[half:]
        wide[:, 2 * step, :] = lane_join(low[:, :BLK], high[:, :BLK])
        wide[:, 2 * step + 1, :] = lane_join(low[:, BLK:], high[:, BLK:])
    out_ref[...] = wide[...].astype(jnp.bfloat16)


def pack_pairs(tile_rows, moment_one, moment_two, delay):
    half = tile_rows.shape[0] // 2
    vmem = pl.BlockSpec(memory_space=pltpu.VMEM)
    return pl.pallas_call(
        pack_kernel,
        out_shape=jax.ShapeDtypeStruct((half, BLK, 2 * BLK), jnp.bfloat16),
        in_specs=[pl.BlockSpec(memory_space=pltpu.SMEM)] + [vmem] * 3,
        out_specs=vmem,
        scratch_shapes=[pltpu.VMEM((half, BLK, 2 * BLK), jnp.float32)],
        compiler_params=pltpu.CompilerParams(vmem_limit_bytes=VMEM_BYTES),
        name="pack",
    )(delay, tile_rows, moment_one, moment_two)


def unpack_kernel(pairs_ref, out_ref, wide):
    half = pairs_ref.shape[0]
    wide[...] = pairs_ref[...].astype(jnp.float32)
    for step in range(BLK // 2):
        at = slice(step * 2 * BLK, (step + 1) * 2 * BLK)
        even, odd = wide[:, 2 * step, :], wide[:, 2 * step + 1, :]
        out_ref[:half, at] = lane_join(even[:, :BLK], odd[:, :BLK])
        out_ref[half:, at] = lane_join(even[:, BLK:], odd[:, BLK:])


def unpack_pairs(pairs):
    half = pairs.shape[0]
    vmem = pl.BlockSpec(memory_space=pltpu.VMEM)
    return pl.pallas_call(
        unpack_kernel,
        out_shape=jax.ShapeDtypeStruct((2 * half, BLK * BLK), jnp.float32),
        in_specs=[vmem],
        out_specs=vmem,
        scratch_shapes=[pltpu.VMEM((half, BLK, 2 * BLK), jnp.float32)],
        compiler_params=pltpu.CompilerParams(vmem_limit_bytes=VMEM_BYTES),
        name="unpack",
    )(pairs)


def swap_halves(value):
    return jnp.concatenate([value[:, BLK:], value[:, :BLK]], axis=1)


def lane_half():
    return lax.broadcasted_iota(jnp.int32, (BLK, 2 * BLK), 1) // BLK


def block_numbers(pair, half):
    first = (pair // half) * (2 * half) + pair % half
    return (first, first + half)


def assemble_kernel(half, rows_ref, cols_ref, pairs_ref, out_ref):
    @pl.loop(0, D // 512)
    def _(chunk):
        out_ref[pl.ds(pl.multiple_of(chunk * 512, 512), 512), :] = jnp.zeros((512, R), jnp.bfloat16)

    @pl.loop(0, pairs_ref.shape[0], unroll=4)
    def _(pair):
        straight = pairs_ref[pair]
        swapped = swap_halves(straight)
        for side, number in enumerate(block_numbers(pair, half)):
            row, col = rows_ref[number], cols_ref[number]
            parity = col % 2
            at = (
                pl.ds(pl.multiple_of(row * BLK, BLK), BLK),
                pl.ds(pl.multiple_of((col // 2) * 2 * BLK, 2 * BLK), 2 * BLK),
            )
            tile = jnp.where(parity == side, straight, swapped)
            out_ref[at] = jnp.where(lane_half() == parity, tile, out_ref[at])


def assemble(pairs, row_pick, col_pick, half):
    return pl.pallas_call(
        functools.partial(assemble_kernel, half),
        out_shape=jax.ShapeDtypeStruct((D, R), jnp.bfloat16),
        in_specs=[pl.BlockSpec(memory_space=pltpu.SMEM)] * 2
        + [pl.BlockSpec(memory_space=pltpu.VMEM)],
        out_specs=pl.BlockSpec(memory_space=pltpu.VMEM),
        compiler_params=pltpu.CompilerParams(vmem_limit_bytes=VMEM_BYTES),
        name="assemble",
    )(row_pick, col_pick, pairs)


def grads_kernel(half, rows_ref, cols_ref, left_ref, right_ref, out_ref, dense):
    @pl.loop(0, D // 512)
    def _(chunk):
        at = pl.ds(pl.multiple_of(chunk * 512, 512), 512)
        dense[at, :] = lax.dot_general(
            left_ref[:, at],
            right_ref[...],
            (((0,), (0,)), ((), ())),
            preferred_element_type=jnp.float32,
        ).astype(jnp.bfloat16)

    @pl.loop(0, out_ref.shape[0], unroll=4)
    def _(pair):
        tiles = []
        for side, number in enumerate(block_numbers(pair, half)):
            row, col = rows_ref[number], cols_ref[number]
            tile = dense[
                pl.ds(pl.multiple_of(row * BLK, BLK), BLK),
                pl.ds(pl.multiple_of((col // 2) * 2 * BLK, 2 * BLK), 2 * BLK),
            ]
            tiles.append(jnp.where(col % 2 == side, tile, swap_halves(tile)))
        out_ref[pair] = jnp.where(lane_half() == 0, tiles[0], tiles[1])


def block_grads(left_cat, right_cat, row_pick, col_pick, half):
    pairs = row_pick.shape[0] // 2
    return pl.pallas_call(
        functools.partial(grads_kernel, half),
        out_shape=jax.ShapeDtypeStruct((pairs, BLK, 2 * BLK), jnp.bfloat16),
        in_specs=[pl.BlockSpec(memory_space=pltpu.SMEM)] * 2
        + [pl.BlockSpec(memory_space=pltpu.VMEM)] * 2,
        out_specs=pl.BlockSpec(memory_space=pltpu.VMEM),
        scratch_shapes=[pltpu.VMEM((D, R), jnp.bfloat16)],
        compiler_params=pltpu.CompilerParams(vmem_limit_bytes=VMEM_BYTES),
        name="block_grads",
    )(row_pick, col_pick, left_cat, right_cat)


def relay_kernel(
    phases,
    inputs_ref,
    cotangent_ref,
    gain_ref,
    matrix_ref,
    left_ref,
    right_ref,
    total_ref,
    x_in,
    x_out,
    grad_back,
    pre_all,
    scale_all,
    sums,
    square,
    send_sem,
    recv_sem,
):
    micro_count, tok_rows, width = inputs_ref.shape
    chunks = width // CHUNK
    phase_id = lax.axis_index("phase")
    has_next, has_prev = (phase_id < phases - 1, phase_id > 0)
    after, before = (lax.rem(phase_id + 1, phases), lax.rem(phase_id + phases - 1, phases))
    barrier = pltpu.get_barrier_semaphore()

    for neighbour in (after, before):
        pl.semaphore_signal(
            barrier, inc=1, device_id={"phase": neighbour}, device_id_type=pl.DeviceIdType.MESH
        )

    def span(chunk):
        return pl.ds(pl.multiple_of(chunk * CHUNK, CHUNK), CHUNK)

    def grad_rows(batch):
        return pl.ds((micro_count + batch) * tok_rows, tok_rows)

    def batch_rows(batch):
        return pl.ds(batch * tok_rows, tok_rows)

    def forward_copy(batch, chunk):
        return pltpu.make_async_remote_copy(
            src_ref=x_out.at[batch, :, span(chunk)],
            dst_ref=x_in.at[batch, :, span(chunk)],
            send_sem=send_sem.at[0, batch, chunk],
            recv_sem=recv_sem.at[0, batch, chunk],
            device_id={"phase": after},
            device_id_type=pl.DeviceIdType.MESH,
        )

    def backward_copy(batch, chunk):
        return pltpu.make_async_remote_copy(
            src_ref=x_out.at[micro_count + batch, :, span(chunk)],
            dst_ref=grad_back.at[batch, :, span(chunk)],
            send_sem=send_sem.at[1, batch, chunk],
            recv_sem=recv_sem.at[1, batch, chunk],
            device_id={"phase": before},
            device_id_type=pl.DeviceIdType.MESH,
        )

    @pl.when(jnp.logical_not(has_prev))
    def _():
        x_in[...] = inputs_ref[...]

    @pl.when(jnp.logical_not(has_next))
    def _():
        grad_back[...] = cotangent_ref[...]

    pl.semaphore_wait(barrier, 2)

    for batch in range(micro_count):
        sums[...] = jnp.zeros_like(sums)
        square[...] = jnp.zeros_like(square)

        @pl.loop(0, chunks)
        def _(chunk):
            @pl.when(has_prev)
            def _():
                forward_copy(batch, chunk).wait_recv()

            at = span(chunk)
            x_float = x_in[batch, :, at].astype(jnp.float32)
            weighted = (x_float * gain_ref[:, at]).astype(jnp.bfloat16)
            square[...] += jnp.sum(x_float * x_float, axis=-1, keepdims=True)
            sums[...] += jnp.dot(weighted, matrix_ref[at, :], preferred_element_type=jnp.float32)

        rms_scale = lax.rsqrt(square[...] / width + norm_epsilon)
        pre = sums[...] * rms_scale
        act = (pre / (1.0 + jnp.exp(-pre))).astype(jnp.bfloat16)
        scale_all[batch] = rms_scale
        pre_all[batch] = pre
        right_ref[grad_rows(batch), :] = act

        @pl.when(has_next)
        def _():
            @pl.loop(0, chunks)
            def _(chunk):
                at = span(chunk)
                moved = transpose_product(right_ref[grad_rows(batch), :], matrix_ref[at, :])
                x_out[batch, :, at] = (x_in[batch, :, at].astype(jnp.float32) + moved).astype(
                    jnp.bfloat16
                )
                forward_copy(batch, chunk).start()

    for batch in range(micro_count):
        sums[...] = jnp.zeros_like(sums)

        @pl.loop(0, chunks)
        def _(chunk):
            @pl.when(has_next)
            def _():
                backward_copy(batch, chunk).wait_recv()

            at = span(chunk)
            sums[...] += jnp.dot(
                grad_back[batch, :, at], matrix_ref[at, :], preferred_element_type=jnp.float32
            )

        pre = pre_all[batch]
        sigmoid_pre = 1.0 / (1.0 + jnp.exp(-pre))
        dpre = (sums[...] * sigmoid_pre * (1.0 + pre * (1.0 - sigmoid_pre))).astype(jnp.bfloat16)
        right_ref[batch_rows(batch), :] = dpre
        inner = jnp.sum(dpre.astype(jnp.float32) * pre, axis=-1, keepdims=True) / width
        square[...] = inner

        @pl.loop(0, chunks)
        def _(chunk):
            at = span(chunk)
            dhidden = transpose_product(right_ref[batch_rows(batch), :], matrix_ref[at, :])
            gain_row = gain_ref[:, at]
            rms_scale = scale_all[batch]
            normed = x_in[batch, :, at].astype(jnp.float32) * rms_scale
            grad_out = grad_back[batch, :, at]
            x_out[micro_count + batch, :, at] = (
                grad_out.astype(jnp.float32)
                + rms_scale * (dhidden * gain_row - normed * square[...])
            ).astype(jnp.bfloat16)

            @pl.when(has_prev)
            def _():
                backward_copy(batch, chunk).start()

            gain_part = jnp.sum(dhidden * normed, axis=0, keepdims=True)
            if batch == 0:
                total_ref[:, at] = gain_part
            else:
                total_ref[:, at] += gain_part
            left_ref[batch_rows(batch), at] = (normed * gain_row).astype(jnp.bfloat16)
            left_ref[grad_rows(batch), at] = grad_out

    @pl.loop(0, chunks)
    def _(chunk):
        for batch in range(micro_count):
            @pl.when(has_next)
            def _():
                forward_copy(batch, chunk).wait_send()

            @pl.when(has_prev)
            def _():
                backward_copy(batch, chunk).wait_send()


def relay(inputs, cotangent, norm_gain, matrix):
    micro_count, tok_rows, width = inputs.shape
    inner = matrix.shape[1]
    vmem = pl.BlockSpec(memory_space=pltpu.VMEM)
    rows = 2 * micro_count * tok_rows
    return pl.pallas_call(
        functools.partial(relay_kernel, lax.axis_size("phase")),
        out_shape=(
            jax.ShapeDtypeStruct((rows, width), jnp.bfloat16),
            jax.ShapeDtypeStruct((rows, inner), jnp.bfloat16),
            jax.ShapeDtypeStruct((1, width), jnp.float32),
        ),
        in_specs=[vmem] * 4,
        out_specs=(vmem,) * 3,
        scratch_shapes=[
            pltpu.VMEM((micro_count, tok_rows, width), jnp.bfloat16),
            pltpu.VMEM((2 * micro_count, tok_rows, width), jnp.bfloat16),
            pltpu.VMEM((micro_count, tok_rows, width), jnp.bfloat16),
            pltpu.VMEM((micro_count, tok_rows, inner), jnp.float32),
            pltpu.VMEM((micro_count, tok_rows, 1), jnp.float32),
            pltpu.VMEM((tok_rows, inner), jnp.float32),
            pltpu.VMEM((tok_rows, 1), jnp.float32),
            pltpu.SemaphoreType.DMA((2, micro_count, width // CHUNK)),
            pltpu.SemaphoreType.DMA((2, micro_count, width // CHUNK)),
        ],
        compiler_params=pltpu.CompilerParams(
            vmem_limit_bytes=VMEM_BYTES, collective_id=0, has_side_effects=True
        ),
        name="relay",
    )(inputs, cotangent, norm_gain, matrix)


def transpose_product(left_side, matrix):
    return lax.dot_general(
        left_side, matrix, (((1,), (1,)), ((), ())), preferred_element_type=jnp.float32
    )


def shards(
    inputs, cotangent, norm_gain, blocks, first_moment, second_moment, row_index, col_index, delays
):
    half = blocks.shape[1] // 2
    local_pairs = pack_pairs(blocks[0], first_moment[0], second_moment[0], delays)
    all_pairs = lax.all_gather(local_pairs, "fsdp", axis=0, tiled=True)
    positions = lax.all_gather(
        jnp.stack([row_index[0], col_index[0]]), "fsdp", axis=1, tiled=True
    )
    all_rows, all_cols = positions[0], positions[1]
    matrix = assemble(all_pairs, all_rows, all_cols, half)
    left_cat, right_cat, gain_total = relay(inputs, cotangent, norm_gain, matrix)
    parts = block_grads(left_cat, right_cat, all_rows, all_cols, half)
    weight_pairs = lax.psum_scatter(parts, "fsdp", scatter_dimension=0, tiled=True)
    weight_part = unpack_pairs(weight_pairs)
    gain_part = lax.psum(gain_total[0].astype(jnp.bfloat16), "fsdp").astype(jnp.float32)
    return (weight_part[None], gain_part[None])


def solution(mesh):
    in_specs = (
        P(None, "fsdp", None),
        P(None, "fsdp", None),
        P("phase", None),
        P("phase", "fsdp", None),
        P("phase", "fsdp", None),
        P("phase", "fsdp", None),
        P("phase", "fsdp"),
        P("phase", "fsdp"),
        P("phase"),
    )
    out_specs = (P("phase", "fsdp", None), P("phase", None))
    return jax.shard_map(shards, mesh=mesh, in_specs=in_specs, out_specs=out_specs, check_vma=False)
```
